32 devices in a mesh: dom: 2 (over x), tm: 16 (over z, y, core).
Axes of the slice: x: 2, y: 2, z: 4, core: 2. Of those that a mesh axis runs over, the one named last changes fastest.
Arguments:
- blocks: float32 [24576, 768], P(('dom', 'tm')), parts along dimension 0, as said below
- couplings: float32 [24576, 768], P(('dom', 'tm')), parts along dimension 0, as said below
- source: float32 [32, 768], P(('dom', 'tm')), parts along dimension 0, may hold values from -6 to 6
Outputs:
- reduced_diag: float32 [24576, 768], P(('dom', 'tm')), parts along dimension 0
- reduced_link: float32 [24576, 768], P(('dom', 'tm')), parts along dimension 0
- reduced_rhs: float32 [32, 768], P(('dom', 'tm')), parts along dimension 0
The draws below stay inside these ranges and needn't reach their ends.
There are 2 independent parts, one for each index of `dom`. The reference program is written for one: setup_inputs(seed, part) draws one part's arguments, and reference() takes and returns one part's arrays. A program takes and returns all parts, laid end to end along the dimension named above; each array names one. Nothing has to cross between parts.
Inputs may be any that keep to these rules, and one draw needn't show every extreme that they name: Every diagonal block is symmetric, and the cyclic block-tridiagonal matrix built from blocks and couplings is positive definite. The couplings are general square blocks, not symmetric; together with blocks they form a positive definite cyclic block-tridiagonal matrix.
All inputs are finite; a program needn't handle non-finite values.
Results may differ from the reference program's by a relative error of at most 0.0003.
Values sent between devices are 32-bit elements; how exact they have to be, the bound alone decides.
A program may use at most 128 MiB of HBM per device.

```python
import jax
import jax.numpy as jnp
from jax import lax

NODES = 768
LEVELS = 2
TIMES = 16


def assemble(key):
    precise = lax.Precision.HIGHEST
    subkeys = [jax.random.fold_in(key, salt) for salt in (101, 102, 103, 104, 105)]
    noise_scale = 0.5 / jnp.sqrt(jnp.float32(NODES))
    identity = jnp.eye(NODES, dtype=jnp.float32)
    forward = jax.random.uniform(subkeys[0], (TIMES, NODES), jnp.float32, 0.1, 1.4)[:, :, None] * identity
    forward = forward + noise_scale * jax.random.normal(subkeys[1], (TIMES, NODES, NODES), jnp.float32)
    backward = jax.random.uniform(subkeys[2], (TIMES, NODES), jnp.float32, 0.1, 1.4)[:, :, None] * identity
    backward = backward + noise_scale * jax.random.normal(subkeys[3], (TIMES, NODES, NODES), jnp.float32)
    shifted = jnp.roll(backward, -1, axis=0)
    diagonal = jnp.einsum('tki,tkj->tij', forward, forward, precision=precise)
    diagonal = diagonal + jnp.einsum('tki,tkj->tij', shifted, shifted, precision=precise) + 0.02 * identity
    coupled = -jnp.einsum('tki,tkj->tij', forward, backward, precision=precise)
    diagonal = 0.5 * (diagonal + jnp.transpose(diagonal, (0, 2, 1)))
    return (diagonal.reshape(TIMES * NODES, NODES), coupled.reshape(TIMES * NODES, NODES))


def draw_blocks(key, part):
    return assemble(key)[0]


def draw_couplings(key, part):
    return assemble(key)[1]


def shard_levels(own_key, shape, shards, least, high):
    gain, own = 1.0, jax.random.fold_in(own_key, 6)
    for dim, shards_of in shards:
        heights = jnp.exp(jax.random.uniform(jax.random.fold_in(own, dim), (shards_of,), jnp.float32, least / len(shards), high / len(shards)))
        gain = gain * jnp.repeat(heights, shape[dim] // shards_of).reshape([-1 if axis == dim else 1 for axis in range(len(shape))])
    return gain


def centred(rng, shape, scale, most, cuts=(), held_as=jnp.bfloat16):
    loudness = shard_levels(rng, shape, cuts, -0.22, 0.18) if cuts else 1.0
    array = jax.random.normal(rng, shape, jnp.float32) * scale * loudness
    return jnp.minimum(jnp.maximum(array, -most), most).astype(held_as)


def setup_inputs(seed: int = 0, part: int = 0) -> dict:
    seeds = jax.random.split(jax.random.key(seed), 4)
    own_keys = jax.random.split(jax.random.fold_in(seeds[3], part), 4)
    blocks = draw_blocks(jax.random.fold_in(jax.random.fold_in(seeds[3], part), 71), part)
    couplings = draw_couplings(jax.random.fold_in(jax.random.fold_in(seeds[3], part), 71), part)
    source = centred(own_keys[2], (TIMES, NODES), 1.0, 6.0, ((0, 16),), jnp.float32)
    return {"blocks": blocks, "couplings": couplings, "source": source}


precise = lax.Precision.HIGHEST

def batched_solve(factor, matrix):
    return jax.vmap(lambda left, right: jax.scipy.linalg.solve_triangular(left, right, lower=True))(factor, matrix)

def inner(former, latter):
    return jnp.einsum('tki,tkj->tij', former, latter, precision=precise)

def halved(matrix):
    return 0.5 * (matrix + jnp.transpose(matrix, (0, 2, 1)))

def reference(blocks, couplings, source):
    spatial = blocks.shape[1]
    times = source.shape[0]
    diagonal = blocks.reshape(times, spatial, spatial)
    coupling = couplings.reshape(times, spatial, spatial)
    vector = source
    for rounds in range(LEVELS):
        stride = 2 ** rounds
        factor = jnp.linalg.cholesky(diagonal)
        whitened = batched_solve(factor, coupling)
        scaled = batched_solve(factor, vector[:, :, None])[:, :, 0]
        gram_block = halved(inner(whitened, whitened))
        gram_vector = jnp.einsum('tki,tk->ti', whitened, scaled, precision=precise)
        upward = batched_solve(jnp.roll(factor, stride, axis=0), jnp.transpose(coupling, (0, 2, 1)))
        lower_gram = halved(inner(upward, upward))
        new_coupling = -inner(upward, jnp.roll(whitened, stride, axis=0))
        lower_vector = jnp.einsum('tki,tk->ti', upward, jnp.roll(scaled, stride, axis=0), precision=precise)
        diagonal = diagonal - lower_gram - jnp.roll(gram_block, -stride, axis=0)
        coupling = new_coupling
        vector = vector - lower_vector - jnp.roll(gram_vector, -stride, axis=0)
    return (diagonal.reshape(times * spatial, spatial), coupling.reshape(times * spatial, spatial), vector)
```

```python
import functools

import jax
import jax.numpy as jnp
from jax import lax
from jax.experimental import pallas as pl
from jax.experimental.pallas import tpu as pltpu
from jax.sharding import PartitionSpec as P

LEVELS = 2
BLOCK = 128
GROUP = 8

precise = lax.Precision.HIGHEST


def passed_along(value, axis, steps):
    count = lax.axis_size(axis)
    pairs = [(source, (source + steps) % count) for source in range(count)]
    return lax.ppermute(value, axis, pairs)


def symmetric(matrix):
    return 0.5 * (matrix + matrix.T)


def product(former, latter):
    return jnp.dot(former, latter, precision=precise)


def three_parts(value):
    high = value.astype(jnp.bfloat16).astype(jnp.float32)
    rest = value - high
    middle = rest.astype(jnp.bfloat16).astype(jnp.float32)
    return high, middle, rest - middle


def gram_of_rows(rows):
    high, middle, low = three_parts(rows)
    former = jnp.concatenate([high, high, middle, high, low, middle], axis=0).astype(jnp.bfloat16)
    latter = jnp.concatenate([high, middle, high, low, high, middle], axis=0).astype(jnp.bfloat16)
    return lax.dot_general(former, latter, (((0,), (0,)), ((), ())), preferred_element_type=jnp.float32)


def inverse_factor(block):
    count = BLOCK // GROUP
    lane = lax.broadcasted_iota(jnp.int32, (GROUP, BLOCK), 1)
    row = lax.broadcasted_iota(jnp.int32, (GROUP, BLOCK), 0)
    groups = [block[GROUP * g : GROUP * (g + 1), :] for g in range(count)]
    done = []
    for g in range(count):
        rows = groups[g]
        start = GROUP * g
        inside = (lane >= start) & (lane < start + GROUP)
        columns = [
            jnp.broadcast_to(rows[:, start + j : start + j + 1], (GROUP, BLOCK)) for j in range(GROUP)
        ]
        rows = jnp.where(inside, jnp.where(lane == row + start, 1.0, 0.0), rows)
        scale = jnp.zeros((GROUP, BLOCK), jnp.float32)
        for j in range(GROUP):
            pivot = jnp.broadcast_to(columns[j][j : j + 1, :], (GROUP, BLOCK))
            root = lax.rsqrt(pivot)
            root = root * (1.5 - 0.5 * (pivot * root) * root)
            scale = jnp.where(row == j, root, scale)
            if j < GROUP - 1:
                factor = jnp.where(row > j, (columns[j] * root) * root, 0.0)
                for k in range(j + 1, GROUP):
                    columns[k] = columns[k] - factor * jnp.broadcast_to(columns[k][j : j + 1, :], (GROUP, BLOCK))
                rows = rows - factor * jnp.broadcast_to(rows[j : j + 1, :], (GROUP, BLOCK))
        rows = rows * scale
        done.append(jnp.where(lane <= row + start, rows, 0.0))
        if g < count - 1:
            update = gram_of_rows(rows)
            for h in range(g + 1, count):
                groups[h] = jnp.where(inside, 0.0, groups[h]) - update[GROUP * h : GROUP * (h + 1), :]
    return jnp.concatenate(done, axis=0)


def factor_kernel(matrix_ref, packed_ref, work):
    size = matrix_ref.shape[0]
    count = size // BLOCK
    work[...] = matrix_ref[...]
    for p in range(count):
        start, stop = p * BLOCK, (p + 1) * BLOCK
        inverse = inverse_factor(work[start:stop, start:stop])
        pieces = [inverse]
        if start:
            pieces.insert(0, product(inverse, work[start:stop, :start]))
        if stop < size:
            pieces.append(product(inverse, work[start:stop, stop:]))
        rows = pieces[0] if len(pieces) == 1 else jnp.concatenate(pieces, axis=1)
        mirror = count - 1 - p
        if p >= mirror:
            packed_ref[mirror * BLOCK : (mirror + 1) * BLOCK, :stop] = rows[:, :stop]
        else:
            packed_ref[start:stop, size - start :] = rows[:, :stop]
        for i in range(p + 1, count):
            first, last = i * BLOCK, (i + 1) * BLOCK
            change = lax.dot_general(
                rows[:, first:last],
                jnp.concatenate([rows[:, :stop], rows[:, first:]], axis=1),
                (((0,), (0,)), ((), ())),
                precision=precise,
                preferred_element_type=jnp.float32,
            )
            if start:
                work[first:last, :start] = work[first:last, :start] - change[:, :start]
            work[first:last, start:stop] = -change[:, start:stop]
            work[first:last, first:] = work[first:last, first:] - change[:, stop:]


def inverse_factor_packed(matrix):
    size = matrix.shape[0]
    return pl.pallas_call(
        factor_kernel,
        out_shape=jax.ShapeDtypeStruct((size // 2, size + BLOCK), jnp.float32),
        in_specs=[pl.BlockSpec(memory_space=pltpu.VMEM)],
        out_specs=pl.BlockSpec(memory_space=pltpu.VMEM),
        scratch_shapes=[pltpu.VMEM((size, size), jnp.float32)],
        compiler_params=pltpu.CompilerParams(vmem_limit_bytes=32 * 2**20),
        cost_estimate=pl.CostEstimate(flops=100 * size**3, bytes_accessed=6 * size**2, transcendentals=0),
    )(matrix)


def unpacked(packed):
    half, wide = packed.shape
    size = 2 * half
    count = size // BLOCK
    block_rows = []
    for p in range(count):
        mirror = count - 1 - p
        stop = (p + 1) * BLOCK
        if p >= mirror:
            block_row = packed[mirror * BLOCK : (mirror + 1) * BLOCK, :stop]
        else:
            block_row = packed[p * BLOCK : stop, size - p * BLOCK :]
        block_rows.append(jnp.pad(block_row, ((0, 0), (0, size - stop))))
    return jnp.concatenate(block_rows, axis=0)


def local(blocks, couplings, source):
    diagonal = blocks
    coupling = couplings
    vector = source[0]
    for rounds in range(LEVELS):
        stride = 2**rounds
        lower_coupling = passed_along(coupling, "tm", stride)
        upper_coupling = passed_along(coupling, "tm", -stride)
        lower_vector = passed_along(vector, "tm", stride)
        upper_vector = passed_along(vector, "tm", -stride)
        packed = inverse_factor_packed(diagonal)
        lower_inverse = unpacked(passed_along(packed, "tm", stride))
        upper_inverse = unpacked(passed_along(packed, "tm", -stride))
        upward = product(lower_inverse, coupling.T)
        lower_whitened = product(lower_inverse, lower_coupling)
        upper_whitened = product(upper_inverse, upper_coupling)
        diagonal = (
            diagonal
            - symmetric(product(upward.T, upward))
            - symmetric(product(upper_whitened.T, upper_whitened))
        )
        coupling = -product(upward.T, lower_whitened)
        vector = (
            vector
            - product(upward.T, product(lower_inverse, lower_vector))
            - product(upper_whitened.T, product(upper_inverse, upper_vector))
        )
    return (diagonal, coupling, vector[None, :])


def solution(mesh):
    placed = (P(("dom", "tm"), None), P(("dom", "tm"), None), P(("dom", "tm"), None))
    return jax.shard_map(
        local,
        mesh=mesh,
        in_specs=placed,
        out_specs=(P(("dom", "tm"), None), P(("dom", "tm"), None), P(("dom", "tm"), None)),
        check_vma=False,
    )
```
